256 devices in a mesh: dp: 16 (over x, y), tensor: 16 (over z, core).
Axes of the slice: x: 4, y: 4, z: 8, core: 2. Of those that a mesh axis runs over, the one named last changes fastest.
Arguments:
- acts: bfloat16 [32, 512, 16384], P('dp', None, 'tensor'), may hold values from -6 to 6
- grads: bfloat16 [32, 512, 53248], P('dp', None, 'tensor'), may hold values from -6 to 6
- proj_in: bfloat16 [16384, 64], P('tensor'), may hold values from -0.046875 to 0.046875
- proj_out: bfloat16 [53248, 64], P('tensor'), may hold values from -0.02734375 to 0.02734375
- lengths: int32 [32], P('dp'), may hold values from 64 to 512, as said below
- queries: int32 [16], replicated, may hold values from 0 to 31, as said below
Outputs:
- blocks: float32 [32, 4096], P('dp', 'tensor')
- scores: float32 [32, 16], P('dp')
The draws below stay inside these ranges and needn't reach their ends.
Inputs may be any that keep to these rules, and one draw needn't show every extreme that they name: `lengths`: some example has exactly 512 tokens in use and some exactly 64. `queries`: all distinct; 0 and 31 are among them.
All inputs are finite; a program needn't handle non-finite values.
Results may differ from the reference program's by a relative error of at most 0.0003.
Values sent between devices are 32-bit elements; how exact they have to be, the bound alone decides.
No kernel may reach another device: no remote copies, remote signals or barrier semaphores. Data moves between devices by JAX's collectives and lax.ppermute only.
A program may use at most 64 MiB of HBM per device.

```python
import jax
import jax.numpy as jnp
from jax import lax

D = 16384
FF = 53248
K = 64
SEQ = 512
EXAMPLES = 32
NQ = 16


def draw_lengths(key, part):
    key = jax.random.fold_in(key, 11)
    first, second = jax.random.split(key)
    counts = jax.random.randint(first, (EXAMPLES,), SEQ // 8, SEQ + 1)
    where_long = jax.random.randint(second, (), 0, EXAMPLES)
    counts = counts.at[where_long].set(SEQ)
    counts = counts.at[(where_long + 1) % EXAMPLES].set(SEQ // 8)
    return counts.astype(jnp.int32)


def draw_queries(key, part):
    key = jax.random.fold_in(key, 23)
    first, second = jax.random.split(key)
    middle = 1 + jax.random.permutation(first, EXAMPLES - 2)[:NQ - 2]
    picked = jnp.concatenate([jnp.zeros((1,), jnp.int32), jnp.full((1,), EXAMPLES - 1, jnp.int32), middle.astype(jnp.int32)])
    order = jax.random.permutation(second, NQ)
    return picked[order].astype(jnp.int32)


def levels(own_key, dims, pieces, least, largest):
    level = 1.0
    for dim, blocks in pieces:
        draws = jax.random.uniform(jax.random.fold_in(jax.random.fold_in(own_key, 6), dim), (blocks,), jnp.float32, least / len(pieces), largest / len(pieces))
        level = level * jnp.repeat(jnp.exp(draws), dims[dim] // blocks).reshape((-1,) + (1,) * (len(dims) - 1 - dim))
    return level


def gaussian(key, extent, scale, bound, shards=(), held_as=jnp.bfloat16):
    entries = scale * jax.random.normal(key, extent, jnp.float32)
    if shards:
        entries = entries * levels(key, extent, shards, -0.22, 0.18)
    return jnp.clip(entries, -bound, bound).astype(held_as)


def setup_inputs(seed: int = 0) -> dict:
    keys = jax.random.split(jax.random.key(seed), 7)
    return {
        "acts": gaussian(keys[0], (EXAMPLES, SEQ, D), 1.0, 6.0, ((0, 16), (2, 16))),
        "grads": gaussian(keys[1], (EXAMPLES, SEQ, FF), 1.0, 6.0, ((0, 16), (2, 16))),
        "proj_in": gaussian(keys[2], (D, K), D ** -0.5, 0.046875, ((0, 16),)),
        "proj_out": gaussian(keys[3], (FF, K), FF ** -0.5, 0.02734375, ((0, 16),)),
        "lengths": draw_lengths(jax.random.fold_in(keys[6], 71), 0),
        "queries": draw_queries(jax.random.fold_in(keys[6], 71), 0),
    }


def reference(acts, grads, proj_in, proj_out, lengths, queries):
    scale = SEQ ** -0.5

    def one_example(items):
        act_rows, grad_rows, count = items
        in_rows = jnp.dot(act_rows, proj_in, preferred_element_type=jnp.float32)
        out_rows = jnp.dot(grad_rows, proj_out, preferred_element_type=jnp.float32)
        keep = (jnp.arange(SEQ, dtype=jnp.int32) < count).astype(jnp.float32)[:, None]
        return jnp.dot((out_rows * keep).T, in_rows, precision=lax.Precision.HIGHEST) * scale

    blocks = lax.map(one_example, (acts, grads, lengths)).reshape(EXAMPLES, K * K)
    chosen = blocks[queries.astype(jnp.int32)]
    scores = jnp.dot(blocks, chosen.T, precision=lax.Precision.HIGHEST) / K
    return blocks, scores
```

```python
import functools

import jax
import jax.numpy as jnp
from jax import lax
from jax.experimental import pallas as pl
from jax.experimental.pallas import tpu as pltpu
from jax.sharding import Mesh, PartitionSpec as P

F32 = jnp.float32
HIGHEST = lax.Precision.HIGHEST
VMEM_BYTES = 16 * 1024 * 1024
ALL_VMEM = 60 * 1024 * 1024
NT = (((1,), (1,)), ((), ()))
TN = (((0,), (0,)), ((), ()))


def vmem():
    return pl.BlockSpec(memory_space=pltpu.VMEM)


def smem():
    return pl.BlockSpec(memory_space=pltpu.SMEM)


def params(limit=VMEM_BYTES):
    return pltpu.CompilerParams(vmem_limit_bytes=limit)


def project_kernel(which, grads, acts, w_out, w_in, out):
    del which
    left = lax.dot_general(grads[0], w_out[...], NT, preferred_element_type=F32)
    right = lax.dot_general(acts[0], w_in[...], NT, preferred_element_type=F32)
    out[...] = jnp.concatenate([left, right], axis=1)


def project(which, grads, acts, w_out, w_in, tile=128):
    _, seq, width_out = grads.shape
    width_in = acts.shape[2]
    rank = w_out.shape[0]
    return pl.pallas_call(
        project_kernel,
        grid_spec=pltpu.PrefetchScalarGridSpec(
            num_scalar_prefetch=1,
            grid=(seq // tile,),
            in_specs=[
                pl.BlockSpec((1, tile, width_out), lambda r, which: (which[0], r, 0)),
                pl.BlockSpec((1, tile, width_in), lambda r, which: (which[0], r, 0)),
                pl.BlockSpec((rank, width_out), lambda r, which: (0, 0)),
                pl.BlockSpec((rank, width_in), lambda r, which: (0, 0)),
            ],
            out_specs=pl.BlockSpec((tile, 2 * rank), lambda r, which: (r, 0)),
        ),
        out_shape=jax.ShapeDtypeStruct((seq, 2 * rank), F32),
        compiler_params=params(ALL_VMEM),
        cost_estimate=pl.CostEstimate(
            flops=2 * seq * rank * (width_in + width_out),
            bytes_accessed=2 * (seq + rank) * (width_in + width_out) + 8 * seq * rank,
            transcendentals=0,
        ),
        name="project",
    )(which, grads, acts, w_out, w_in)


def outer_kernel(scale, count, pieces, out, square):
    rows = jnp.sum(pieces[...], axis=0)
    tokens, width = rows.shape
    rank = width // 2
    keep = (lax.broadcasted_iota(jnp.int32, (tokens, rank), 0) < count[0]).astype(F32)
    square[...] = scale * lax.dot_general(
        rows[:, :rank] * keep, rows[:, rank:], TN, precision=HIGHEST, preferred_element_type=F32
    )
    even = square[pl.ds(0, rank // 2, stride=2), :]
    odd = square[pl.ds(1, rank // 2, stride=2), :]
    flat = jnp.concatenate([even, odd], axis=1)
    out[...] = jnp.broadcast_to(flat[None], out.shape)


def outer(count, pieces, scale):
    shards, _, width = pieces.shape
    rank = width // 2
    return pl.pallas_call(
        functools.partial(outer_kernel, scale),
        in_specs=[smem(), vmem()],
        out_specs=vmem(),
        out_shape=jax.ShapeDtypeStruct((shards, rank // 2, width), F32),
        scratch_shapes=[pltpu.VMEM((rank, rank), F32)],
        compiler_params=params(),
        name="outer",
    )(count, pieces)


def total_kernel(pieces, own, copies):
    block = jnp.sum(pieces[...], axis=0)
    own[...] = block
    copies[...] = jnp.broadcast_to(block[None], copies.shape)


def total(pieces, groups):
    _, rows, width = pieces.shape
    return pl.pallas_call(
        total_kernel,
        in_specs=[vmem()],
        out_specs=[vmem(), vmem()],
        out_shape=[
            jax.ShapeDtypeStruct((rows, width), F32),
            jax.ShapeDtypeStruct((groups, rows, width), F32),
        ],
        compiler_params=params(),
        name="total",
    )(pieces)


def score_kernel(place, queries, own, other, gathered, own_blocks, scores):
    core = place[0]
    start = 2 * place[1]
    rank = 2 * own.shape[0]
    mine, theirs = own[...], other[...]
    pair = (jnp.where(core == 0, mine, theirs), jnp.where(core == 0, theirs, mine))
    for e in range(2):
        ref = (own, other)
        first = [r[pl.ds(start, 1), :] for r in ref]
        second = [r[pl.ds(start + 1, 1), :] for r in ref]
        pick = core == e
        own_blocks[pl.ds(e, 1), :] = jnp.concatenate(
            [jnp.where(pick, first[0], first[1]), jnp.where(pick, second[0], second[1])], axis=1
        )
    blocks = gathered[...]
    groups = blocks.shape[0]
    ids = 2 * lax.broadcasted_iota(jnp.int32, (groups, queries.shape[1]), 0) + core
    select = (ids == queries[...]).astype(F32)
    for e in range(2):
        products = jnp.sum(blocks * pair[e][None], axis=1)
        dots = jnp.sum(products, axis=1, keepdims=True)
        scores[pl.ds(e, 1), :] = jnp.sum(dots * select, axis=0, keepdims=True) / rank


def score(place, queries, own, other, gathered):
    width = own.shape[1]
    return pl.pallas_call(
        score_kernel,
        in_specs=[smem(), vmem(), vmem(), vmem(), vmem()],
        out_specs=[vmem(), vmem()],
        out_shape=[
            jax.ShapeDtypeStruct((2, 2 * width), F32),
            jax.ShapeDtypeStruct((2, queries.shape[0]), F32),
        ],
        compiler_params=params(),
        name="score",
    )(place, queries.reshape(1, -1), own, other, gathered)


SWAP = [(0, 1), (1, 0)]


def body(acts, grads, proj_in, proj_out, lengths, queries):
    seq = acts.shape[1]
    core = lax.axis_index("core").astype(jnp.int32)
    z = lax.axis_index("z").astype(jnp.int32)
    depth = lax.axis_size("z")
    groups = lax.axis_size("x") * lax.axis_size("y")
    w_out, w_in = proj_out.T, proj_in.T
    theirs = project((1 - core)[None], grads, acts, w_out, w_in)
    received = lax.ppermute(theirs, "core", SWAP)
    mine = project(core[None], grads, acts, w_out, w_in)
    rows = (mine + received).reshape(depth, seq // depth, mine.shape[1])
    pieces = lax.all_to_all(rows, "z", 0, 0)
    count = (jnp.where(core == 0, lengths[0], lengths[1]) - z * (seq // depth))[None]
    spread = outer(count, pieces, seq ** (-0.5))
    parts = lax.all_to_all(spread, "z", 0, 0)
    own, copies = total(parts, groups)
    other = lax.ppermute(own, "core", SWAP)
    gathered = lax.all_to_all(copies, ("x", "y"), 0, 0)
    place = jnp.stack([core, 2 * z + core])
    own_blocks, part = score(place, queries, own, other, gathered)
    scores = part + lax.ppermute(part, "core", SWAP)
    return own_blocks, scores


def solution(mesh):
    devices = mesh.devices.reshape(4, 4, 8, 2)
    dp, tensor = ("x", "y"), ("z", "core")
    return jax.shard_map(
        body,
        mesh=Mesh(devices, dp + tensor),
        in_specs=(
            P(dp, None, tensor),
            P(dp, None, tensor),
            P(tensor, None),
            P(tensor, None),
            P(dp),
            P(),
        ),
        out_specs=(P(dp, tensor), P(dp, None)),
        check_vma=False,
    )
```

```python
import functools

import jax
import jax.numpy as jnp
from jax import lax
from jax.experimental import pallas as pl
from jax.experimental.pallas import tpu as pltpu
from jax.sharding import Mesh, PartitionSpec as P

F32 = jnp.float32
HIGHEST = lax.Precision.HIGHEST
VMEM_BYTES = 24 * 1024 * 1024
NT = (((1,), (1,)), ((), ()))
TN = (((0,), (0,)), ((), ()))


def vmem():
    return pl.BlockSpec(memory_space=pltpu.VMEM)


def params():
    return pltpu.CompilerParams(vmem_limit_bytes=VMEM_BYTES)


def in_hbm(x):
    return pltpu.with_memory_space_constraint(x, pltpu.HBM)


def project_kernel(grads, acts, w_out, w_in, out):
    rank = w_out.shape[0]
    out[:, rank:] = lax.dot_general(acts[0], w_in[...], NT, preferred_element_type=F32)
    out[:, :rank] = lax.dot_general(grads[0], w_out[...], NT, preferred_element_type=F32)


def project(which, grads, acts, w_out, w_in, tile=256):
    _, seq, width_out = grads.shape
    width_in = acts.shape[2]
    rank = w_out.shape[0]
    return pl.pallas_call(
        project_kernel,
        grid=(seq // tile,),
        in_specs=[
            pl.BlockSpec((1, tile, width_out), lambda r: (which(), r, 0)),
            pl.BlockSpec((1, tile, width_in), lambda r: (which(), r, 0)),
            pl.BlockSpec((rank, width_out), lambda r: (0, 0)),
            pl.BlockSpec((rank, width_in), lambda r: (0, 0)),
        ],
        out_specs=pl.BlockSpec((tile, 2 * rank), lambda r: (r, 0)),
        out_shape=jax.ShapeDtypeStruct((seq, 2 * rank), F32),
        compiler_params=params(),
        cost_estimate=pl.CostEstimate(
            flops=2 * seq * rank * (width_in + width_out),
            bytes_accessed=2 * (seq + rank) * (width_in + width_out) + 8 * seq * rank,
            transcendentals=0,
        ),
        name="project",
    )(in_hbm(grads), in_hbm(acts), in_hbm(w_out), in_hbm(w_in))


def outer_kernel(scale, lengths, pieces, out, square):
    rows = jnp.sum(pieces[...], axis=0)
    tokens, width = rows.shape
    rank = width // 2
    core, z = lax.axis_index("core"), lax.axis_index("z")
    count = jnp.where(core == 0, lengths[:, :1], lengths[:, 1:2])
    token = lax.broadcasted_iota(jnp.int32, (tokens, rank), 0) + z * tokens
    keep = (token < count).astype(F32)
    square[...] = scale * lax.dot_general(
        rows[:, :rank] * keep, rows[:, rank:], TN, precision=HIGHEST, preferred_element_type=F32
    )
    even = square[pl.ds(0, rank // 2, stride=2), :]
    odd = square[pl.ds(1, rank // 2, stride=2), :]
    flat = jnp.concatenate([even, odd], axis=1)
    out[...] = jnp.broadcast_to(flat[None], out.shape)


def outer(lengths, pieces, scale):
    shards, _, width = pieces.shape
    rank = width // 2
    return pl.pallas_call(
        functools.partial(outer_kernel, scale),
        in_specs=[vmem(), vmem()],
        out_specs=vmem(),
        out_shape=jax.ShapeDtypeStruct((shards, rank // 2, width), F32),
        scratch_shapes=[pltpu.VMEM((rank, rank), F32)],
        compiler_params=params(),
        name="outer",
    )(lengths.reshape(1, -1), pieces)


def total_kernel(pieces, own):
    own[...] = jnp.sum(pieces[...], axis=0)


def total(pieces):
    return pl.pallas_call(
        total_kernel,
        in_specs=[vmem()],
        out_specs=vmem(),
        out_shape=jax.ShapeDtypeStruct(pieces.shape[1:], F32),
        compiler_params=params(),
        name="total",
    )(pieces)


def keep_kernel(own, other, out):
    core = lax.axis_index("core")
    start = 2 * (2 * lax.axis_index("z") + core)
    first = [r[pl.ds(start, 1), :] for r in (own, other)]
    second = [r[pl.ds(start + 1, 1), :] for r in (own, other)]
    for e in range(2):
        pick = core == e
        out[pl.ds(e, 1), :] = jnp.concatenate(
            [jnp.where(pick, first[0], first[1]), jnp.where(pick, second[0], second[1])], axis=1
        )


def keep_columns(own, other):
    return pl.pallas_call(
        keep_kernel,
        in_specs=[vmem(), vmem()],
        out_specs=vmem(),
        out_shape=jax.ShapeDtypeStruct((2, 2 * own.shape[1]), F32),
        compiler_params=params(),
        name="keep_columns",
    )(own, other)


def score_kernel(queries, own, other, gathered, scores):
    core = lax.axis_index("core")
    rank = 2 * own.shape[0]
    mine, theirs = own[...], other[...]
    pair = (jnp.where(core == 0, mine, theirs), jnp.where(core == 0, theirs, mine))
    blocks = gathered[...]
    groups = blocks.shape[0]
    ids = 2 * lax.broadcasted_iota(jnp.int32, (groups, queries.shape[1]), 0) + core
    select = (ids == queries[...]).astype(F32)
    for e in range(2):
        products = jnp.sum(blocks * pair[e][None], axis=1)
        dots = jnp.sum(products, axis=1, keepdims=True)
        scores[pl.ds(e, 1), :] = jnp.sum(dots * select, axis=0, keepdims=True) / rank


def score(queries, own, other, gathered):
    return pl.pallas_call(
        score_kernel,
        in_specs=[vmem(), vmem(), vmem(), vmem()],
        out_specs=vmem(),
        out_shape=jax.ShapeDtypeStruct((2, queries.shape[0]), F32),
        compiler_params=params(),
        name="score",
    )(queries.reshape(1, -1), own, other, gathered)


SWAP = [(0, 1), (1, 0)]


def body(acts, grads, proj_in, proj_out, lengths, queries):
    seq = acts.shape[1]
    depth = lax.axis_size("z")
    groups = lax.axis_size("x") * lax.axis_size("y")
    w_out, w_in = proj_out.T, proj_in.T
    theirs = project(lambda: 1 - lax.axis_index("core"), grads, acts, w_out, w_in)
    received = lax.ppermute(theirs, "core", SWAP)
    mine = project(lambda: lax.axis_index("core"), grads, acts, w_out, w_in)
    rows = (mine + received).reshape(depth, seq // depth, mine.shape[1])
    pieces = lax.all_to_all(rows, "z", 0, 0)
    spread = outer(lengths, pieces, seq ** (-0.5))
    parts = lax.all_to_all(spread, "z", 0, 0)
    own = total(parts)
    other = lax.ppermute(own, "core", SWAP)
    copies = jnp.broadcast_to(own[None], (groups,) + own.shape)
    gathered = lax.all_to_all(copies, ("x", "y"), 0, 0)
    own_blocks = keep_columns(own, other)
    part = score(queries, own, other, gathered)
    scores = part + lax.ppermute(part, "core", SWAP)
    return own_blocks, scores


def solution(mesh):
    devices = mesh.devices.reshape(4, 4, 8, 2)
    dp, tensor = ("x", "y"), ("z", "core")
    return jax.shard_map(
        body,
        mesh=Mesh(devices, dp + tensor),
        in_specs=(
            P(dp, None, tensor),
            P(dp, None, tensor),
            P(tensor, None),
            P(tensor, None),
            P(dp),
            P(),
        ),
        out_specs=(P(dp, tensor), P(dp, None)),
        check_vma=False,
    )
```

```python
import functools

import jax
import jax.numpy as jnp
from jax import lax
from jax.experimental import pallas as pl
from jax.experimental.pallas import tpu as pltpu
from jax.sharding import Mesh, PartitionSpec as P

F32 = jnp.float32
HIGHEST = lax.Precision.HIGHEST
VMEM_BYTES = 24 * 1024 * 1024
NT = (((1,), (1,)), ((), ()))
TN = (((0,), (0,)), ((), ()))


def vmem():
    return pl.BlockSpec(memory_space=pltpu.VMEM)


def params():
    return pltpu.CompilerParams(vmem_limit_bytes=VMEM_BYTES)


def in_hbm(x):
    return pltpu.with_memory_space_constraint(x, pltpu.HBM)


def project_kernel(grads, acts, w_out, w_in, out):
    rank = w_out.shape[0]
    out[:, rank:] = lax.dot_general(acts[...], w_in[...], NT, preferred_element_type=F32)
    out[:, :rank] = lax.dot_general(grads[...], w_out[...], NT, preferred_element_type=F32)


def project(grads, acts, w_out, w_in, tile):
    rows, width_out = grads.shape
    width_in = acts.shape[1]
    rank = w_out.shape[0]
    return pl.pallas_call(
        project_kernel,
        grid=(rows // tile,),
        in_specs=[
            pl.BlockSpec((tile, width_out), lambda r: (r, 0)),
            pl.BlockSpec((tile, width_in), lambda r: (r, 0)),
            pl.BlockSpec((rank, width_out), lambda r: (0, 0)),
            pl.BlockSpec((rank, width_in), lambda r: (0, 0)),
        ],
        out_specs=pl.BlockSpec((tile, 2 * rank), lambda r: (r, 0)),
        out_shape=jax.ShapeDtypeStruct((rows, 2 * rank), F32),
        compiler_params=params(),
        cost_estimate=pl.CostEstimate(
            flops=2 * rows * rank * (width_in + width_out),
            bytes_accessed=2 * (rows + rank) * (width_in + width_out) + 8 * rows * rank,
            transcendentals=0,
        ),
        name="project",
    )(in_hbm(grads), in_hbm(acts), in_hbm(w_out), in_hbm(w_in))


def outer_kernel(scale, lengths, pieces, out, square):
    rows = jnp.sum(pieces[...], axis=0)
    tokens, width = rows.shape
    rank = width // 2
    core, z = lax.axis_index("core"), lax.axis_index("z")
    count = jnp.where(core == 0, lengths[:, :1], lengths[:, 1:2])
    token = lax.broadcasted_iota(jnp.int32, (tokens, rank), 0) + z * tokens
    keep = (token < count).astype(F32)
    square[...] = scale * lax.dot_general(
        rows[:, :rank] * keep, rows[:, rank:], TN, precision=HIGHEST, preferred_element_type=F32
    )
    even = square[pl.ds(0, rank // 2, stride=2), :]
    odd = square[pl.ds(1, rank // 2, stride=2), :]
    flat = jnp.concatenate([even, odd], axis=1)
    out[...] = jnp.broadcast_to(flat[None], out.shape)


def outer(lengths, pieces, scale):
    shards, _, width = pieces.shape
    rank = width // 2
    return pl.pallas_call(
        functools.partial(outer_kernel, scale),
        in_specs=[vmem(), vmem()],
        out_specs=vmem(),
        out_shape=jax.ShapeDtypeStruct((shards, rank // 2, width), F32),
        scratch_shapes=[pltpu.VMEM((rank, rank), F32)],
        compiler_params=params(),
        name="outer",
    )(lengths.reshape(1, -1), pieces)


def total_kernel(pieces, own):
    own[...] = jnp.sum(pieces[...], axis=0)


def total(pieces):
    return pl.pallas_call(
        total_kernel,
        in_specs=[vmem()],
        out_specs=vmem(),
        out_shape=jax.ShapeDtypeStruct(pieces.shape[1:], F32),
        compiler_params=params(),
        name="total",
    )(pieces)


def finish_kernel(queries, mine, theirs, blocks, scores):
    x, y, z, core = [lax.axis_index(axis) for axis in ("x", "y", "z", "core")]
    groups, rows, _ = mine.shape
    dp = x * lax.axis_size("y") + y
    group = lax.broadcasted_iota(jnp.int32, (groups, queries.shape[1]), 0)
    asked = queries[...]
    select = (2 * group + core == asked).astype(F32)
    select_other = (2 * group + 1 - core == asked).astype(F32)
    first, second = mine[...], theirs[...]
    for e in range(2):
        pick = core == e
        own = jnp.where(pick, mine[dp], theirs[dp])
        dots = jnp.sum(jnp.sum(first * own[None], axis=1), axis=1, keepdims=True)
        other = jnp.sum(jnp.sum(second * own[None], axis=1), axis=1, keepdims=True)
        total = jnp.sum(dots * select + other * select_other, axis=0, keepdims=True)
        scores[pl.ds(e, 1), :] = total / (2 * rows)
        place = 2 * (2 * z + core)
        cut = [
            jnp.where(pick, mine[dp, pl.ds(place + k, 1), :], theirs[dp, pl.ds(place + k, 1), :])
            for k in range(2)
        ]
        blocks[pl.ds(e, 1), :] = jnp.concatenate(cut, axis=1)


def finish(queries, mine, theirs):
    return pl.pallas_call(
        finish_kernel,
        in_specs=[vmem()] * 3,
        out_specs=[vmem()] * 2,
        out_shape=[
            jax.ShapeDtypeStruct((2, 2 * mine.shape[2]), F32),
            jax.ShapeDtypeStruct((2, queries.shape[0]), F32),
        ],
        compiler_params=params(),
        name="finish",
    )(queries.reshape(1, -1), mine, theirs)


SWAP = [(0, 1), (1, 0)]


def body(acts, grads, proj_in, proj_out, lengths, queries):
    seq = acts.shape[1]
    depth = lax.axis_size("z")
    groups = lax.axis_size("x") * lax.axis_size("y")
    core = lax.axis_index("core")
    part = project(
        grads.reshape(-1, grads.shape[2]), acts.reshape(-1, acts.shape[2]), proj_out.T, proj_in.T, seq
    ).reshape(acts.shape[0], seq, -1)
    received = lax.ppermute(lax.dynamic_index_in_dim(part, 1 - core, 0, False), "core", SWAP)
    rows = lax.dynamic_index_in_dim(part, core, 0, False) + received
    rows = rows.reshape(depth, seq // depth, rows.shape[1])
    pieces = lax.all_to_all(rows, "z", 0, 0)
    spread = outer(lengths, pieces, seq ** (-0.5))
    parts = lax.all_to_all(spread, "z", 0, 0)
    own = total(parts)
    copies = jnp.broadcast_to(own[None], (groups,) + own.shape)
    gathered = lax.all_to_all(copies, ("x", "y"), 0, 0)
    received = lax.ppermute(gathered, "core", SWAP)
    return tuple(finish(queries, gathered, received))


def solution(mesh):
    devices = mesh.devices.reshape(4, 4, 8, 2)
    dp, tensor = ("x", "y"), ("z", "core")
    return jax.shard_map(
        body,
        mesh=Mesh(devices, dp + tensor),
        in_specs=(
            P(dp, None, tensor),
            P(dp, None, tensor),
            P(tensor, None),
            P(tensor, None),
            P(dp),
            P(),
        ),
        out_specs=(P(dp, tensor), P(dp, None)),
        check_vma=False,
    )
```

```python
import functools

import jax
import jax.numpy as jnp
from jax import lax
from jax.experimental import pallas as pl
from jax.experimental.pallas import tpu as pltpu
from jax.sharding import Mesh, PartitionSpec as P

F32 = jnp.float32
HIGHEST = lax.Precision.HIGHEST
VMEM_BYTES = 24 * 1024 * 1024
NT = (((1,), (1,)), ((), ()))
TN = (((0,), (0,)), ((), ()))
Z_ORDER = (4, 0, 5, 1, 6, 2, 7, 3)
XY_ORDER = (10, 11, 12, 13, 14, 15, 0, 1, 2, 3, 4, 5, 6, 7, 8, 9)


def place_in(order, index):
    return sum(jnp.where(index == held, place, 0) for place, held in enumerate(order))


def exchange(x, axes, order):
    return lax.all_to_all(x, axes, 0, 0, axis_index_groups=[list(order)])


def vmem():
    return pl.BlockSpec(memory_space=pltpu.VMEM)


def params():
    return pltpu.CompilerParams(vmem_limit_bytes=VMEM_BYTES)


def in_hbm(x):
    return pltpu.with_memory_space_constraint(x, pltpu.HBM)


def project_kernel(grads, acts, w_out, w_in, out):
    rank = w_out.shape[0]
    out[:, rank:] = lax.dot_general(acts[...], w_in[...], NT, preferred_element_type=F32)
    out[:, :rank] = lax.dot_general(grads[...], w_out[...], NT, preferred_element_type=F32)


def project(grads, acts, w_out, w_in, tile):
    rows, width_out = grads.shape
    width_in = acts.shape[1]
    rank = w_out.shape[0]
    return pl.pallas_call(
        project_kernel,
        grid=(rows // tile,),
        in_specs=[
            pl.BlockSpec((tile, width_out), lambda r: (r, 0)),
            pl.BlockSpec((tile, width_in), lambda r: (r, 0)),
            pl.BlockSpec((rank, width_out), lambda r: (0, 0)),
            pl.BlockSpec((rank, width_in), lambda r: (0, 0)),
        ],
        out_specs=pl.BlockSpec((tile, 2 * rank), lambda r: (r, 0)),
        out_shape=jax.ShapeDtypeStruct((rows, 2 * rank), F32),
        compiler_params=params(),
        cost_estimate=pl.CostEstimate(
            flops=2 * rows * rank * (width_in + width_out),
            bytes_accessed=2 * (rows + rank) * (width_in + width_out) + 8 * rows * rank,
            transcendentals=0,
        ),
        name="project",
    )(in_hbm(grads), in_hbm(acts), in_hbm(w_out), in_hbm(w_in))


def outer_kernel(scale, lengths, pieces, out, square):
    rows = jnp.sum(pieces[...], axis=0)
    tokens, width = rows.shape
    rank = width // 2
    core = lax.axis_index("core")
    chunk = place_in(Z_ORDER, lax.axis_index("z"))
    count = jnp.where(core == 0, lengths[:, :1], lengths[:, 1:2])
    token = lax.broadcasted_iota(jnp.int32, (tokens, rank), 0) + chunk * tokens
    keep = (token < count).astype(F32)
    square[...] = scale * lax.dot_general(
        rows[:, :rank] * keep, rows[:, rank:], TN, precision=HIGHEST, preferred_element_type=F32
    )
    even = square[pl.ds(0, rank // 2, stride=2), :]
    odd = square[pl.ds(1, rank // 2, stride=2), :]
    flat = jnp.concatenate([even, odd], axis=1)
    out[...] = jnp.broadcast_to(flat[None], out.shape)


def outer(lengths, pieces, scale):
    shards, _, width = pieces.shape
    rank = width // 2
    return pl.pallas_call(
        functools.partial(outer_kernel, scale),
        in_specs=[vmem(), vmem()],
        out_specs=vmem(),
        out_shape=jax.ShapeDtypeStruct((shards, rank // 2, width), F32),
        scratch_shapes=[pltpu.VMEM((rank, rank), F32)],
        compiler_params=params(),
        name="outer",
    )(lengths.reshape(1, -1), pieces)


def total_kernel(pieces, own):
    own[...] = jnp.sum(pieces[...], axis=0)


def total(pieces):
    return pl.pallas_call(
        total_kernel,
        in_specs=[vmem()],
        out_specs=vmem(),
        out_shape=jax.ShapeDtypeStruct(pieces.shape[1:], F32),
        compiler_params=params(),
        name="total",
    )(pieces)


def finish_kernel(queries, mine, theirs, blocks, scores):
    x, y, z, core = [lax.axis_index(axis) for axis in ("x", "y", "z", "core")]
    groups, rows, _ = mine.shape
    dp = place_in(XY_ORDER, x * lax.axis_size("y") + y)
    shape = (groups, queries.shape[1])
    held = lax.broadcasted_iota(jnp.int32, shape, 0) + XY_ORDER[0]
    group = jnp.where(held >= groups, held - groups, held)
    asked = queries[...]
    select = (2 * group + core == asked).astype(F32)
    select_other = (2 * group + 1 - core == asked).astype(F32)
    first, second = mine[...], theirs[...]
    for e in range(2):
        pick = core == e
        own = jnp.where(pick, mine[dp], theirs[dp])
        dots = jnp.sum(jnp.sum(first * own[None], axis=1), axis=1, keepdims=True)
        other = jnp.sum(jnp.sum(second * own[None], axis=1), axis=1, keepdims=True)
        total = jnp.sum(dots * select + other * select_other, axis=0, keepdims=True)
        scores[pl.ds(e, 1), :] = total / (2 * rows)
        place = 2 * (2 * z + core)
        cut = [
            jnp.where(pick, mine[dp, pl.ds(place + k, 1), :], theirs[dp, pl.ds(place + k, 1), :])
            for k in range(2)
        ]
        blocks[pl.ds(e, 1), :] = jnp.concatenate(cut, axis=1)


def finish(queries, mine, theirs):
    return pl.pallas_call(
        finish_kernel,
        in_specs=[vmem()] * 3,
        out_specs=[vmem()] * 2,
        out_shape=[
            jax.ShapeDtypeStruct((2, 2 * mine.shape[2]), F32),
            jax.ShapeDtypeStruct((2, queries.shape[0]), F32),
        ],
        compiler_params=params(),
        name="finish",
    )(queries.reshape(1, -1), mine, theirs)


SWAP = [(0, 1), (1, 0)]


def body(acts, grads, proj_in, proj_out, lengths, queries):
    seq = acts.shape[1]
    depth = lax.axis_size("z")
    groups = lax.axis_size("x") * lax.axis_size("y")
    core = lax.axis_index("core")
    part = project(
        grads.reshape(-1, grads.shape[2]), acts.reshape(-1, acts.shape[2]), proj_out.T, proj_in.T, seq
    ).reshape(acts.shape[0], seq, -1)
    received = lax.ppermute(lax.dynamic_index_in_dim(part, 1 - core, 0, False), "core", SWAP)
    rows = lax.dynamic_index_in_dim(part, core, 0, False) + received
    rows = rows.reshape(depth, seq // depth, rows.shape[1])
    pieces = exchange(rows, "z", Z_ORDER)
    spread = outer(lengths, pieces, seq ** (-0.5))
    parts = exchange(spread, "z", Z_ORDER)
    own = total(parts)
    copies = jnp.broadcast_to(own[None], (groups,) + own.shape)
    gathered = exchange(copies, ("x", "y"), XY_ORDER)
    received = lax.ppermute(gathered, "core", SWAP)
    return tuple(finish(queries, gathered, received))


def solution(mesh):
    devices = mesh.devices.reshape(4, 4, 8, 2)
    dp, tensor = ("x", "y"), ("z", "core")
    return jax.shard_map(
        body,
        mesh=Mesh(devices, dp + tensor),
        in_specs=(
            P(dp, None, tensor),
            P(dp, None, tensor),
            P(tensor, None),
            P(tensor, None),
            P(dp),
            P(),
        ),
        out_specs=(P(dp, tensor), P(dp, None)),
        check_vma=False,
    )
```

```python
import functools

import jax
import jax.numpy as jnp
from jax import lax
from jax.experimental import pallas as pl
from jax.experimental.pallas import tpu as pltpu
from jax.sharding import Mesh, PartitionSpec as P

F32 = jnp.float32
HIGHEST = lax.Precision.HIGHEST
VMEM_BYTES = 24 * 1024 * 1024
NT = (((1,), (1,)), ((), ()))
TN = (((0,), (0,)), ((), ()))
Z_ORDER = (4, 0, 1, 7, 2, 6, 3, 5)
XY_ORDER = (10, 11, 12, 13, 14, 15, 0, 1, 2, 3, 4, 5, 6, 7, 8, 9)


def place_in(order, index):
    return sum(jnp.where(index == held, place, 0) for place, held in enumerate(order))


def exchange(x, axes, order):
    return lax.all_to_all(x, axes, 0, 0, axis_index_groups=[list(order)])


def vmem():
    return pl.BlockSpec(memory_space=pltpu.VMEM)


def params():
    return pltpu.CompilerParams(vmem_limit_bytes=VMEM_BYTES)


def in_hbm(x):
    return pltpu.with_memory_space_constraint(x, pltpu.HBM)


def project_kernel(grads, acts, w_out, w_in, out):
    rank = w_out.shape[0]
    out[:, rank:] = lax.dot_general(acts[...], w_in[...], NT, preferred_element_type=F32)
    out[:, :rank] = lax.dot_general(grads[...], w_out[...], NT, preferred_element_type=F32)


def project(grads, acts, w_out, w_in, tile):
    rows, width_out = grads.shape
    width_in = acts.shape[1]
    rank = w_out.shape[0]
    return pl.pallas_call(
        project_kernel,
        grid=(rows // tile,),
        in_specs=[
            pl.BlockSpec((tile, width_out), lambda r: (r, 0)),
            pl.BlockSpec((tile, width_in), lambda r: (r, 0)),
            pl.BlockSpec((rank, width_out), lambda r: (0, 0)),
            pl.BlockSpec((rank, width_in), lambda r: (0, 0)),
        ],
        out_specs=pl.BlockSpec((tile, 2 * rank), lambda r: (r, 0)),
        out_shape=jax.ShapeDtypeStruct((rows, 2 * rank), F32),
        compiler_params=params(),
        cost_estimate=pl.CostEstimate(
            flops=2 * rows * rank * (width_in + width_out),
            bytes_accessed=2 * (rows + rank) * (width_in + width_out) + 8 * rows * rank,
            transcendentals=0,
        ),
        name="project",
    )(in_hbm(grads), in_hbm(acts), in_hbm(w_out), in_hbm(w_in))


def outer_kernel(scale, lengths, pieces, out, square):
    rows = jnp.sum(pieces[...], axis=0)
    tokens, width = rows.shape
    rank = width // 2
    core = lax.axis_index("core")
    chunk = place_in(Z_ORDER, lax.axis_index("z"))
    count = jnp.where(core == 0, lengths[:, :1], lengths[:, 1:2])
    token = lax.broadcasted_iota(jnp.int32, (tokens, rank), 0) + chunk * tokens
    keep = (token < count).astype(F32)
    square[...] = scale * lax.dot_general(
        rows[:, :rank] * keep, rows[:, rank:], TN, precision=HIGHEST, preferred_element_type=F32
    )
    even = square[pl.ds(0, rank // 2, stride=2), :]
    odd = square[pl.ds(1, rank // 2, stride=2), :]
    flat = jnp.concatenate([even, odd], axis=1)
    out[...] = jnp.broadcast_to(flat[None], out.shape)


def outer(lengths, pieces, scale):
    shards, _, width = pieces.shape
    rank = width // 2
    return pl.pallas_call(
        functools.partial(outer_kernel, scale),
        in_specs=[vmem(), vmem()],
        out_specs=vmem(),
        out_shape=jax.ShapeDtypeStruct((shards, rank // 2, width), F32),
        scratch_shapes=[pltpu.VMEM((rank, rank), F32)],
        compiler_params=params(),
        name="outer",
    )(lengths.reshape(1, -1), pieces)


def total_kernel(pieces, own):
    own[...] = jnp.sum(pieces[...], axis=0)


def total(pieces):
    return pl.pallas_call(
        total_kernel,
        in_specs=[vmem()],
        out_specs=vmem(),
        out_shape=jax.ShapeDtypeStruct(pieces.shape[1:], F32),
        compiler_params=params(),
        name="total",
    )(pieces)


def finish_kernel(queries, mine, theirs, blocks, scores):
    x, y, z, core = [lax.axis_index(axis) for axis in ("x", "y", "z", "core")]
    groups, rows, _ = mine.shape
    dp = place_in(XY_ORDER, x * lax.axis_size("y") + y)
    shape = (groups, queries.shape[1])
    held = lax.broadcasted_iota(jnp.int32, shape, 0) + XY_ORDER[0]
    group = jnp.where(held >= groups, held - groups, held)
    asked = queries[...]
    select = (2 * group + core == asked).astype(F32)
    select_other = (2 * group + 1 - core == asked).astype(F32)
    first, second = mine[...], theirs[...]
    for e in range(2):
        pick = core == e
        own = jnp.where(pick, mine[dp], theirs[dp])
        dots = jnp.sum(jnp.sum(first * own[None], axis=1), axis=1, keepdims=True)
        other = jnp.sum(jnp.sum(second * own[None], axis=1), axis=1, keepdims=True)
        total = jnp.sum(dots * select + other * select_other, axis=0, keepdims=True)
        scores[pl.ds(e, 1), :] = total / (2 * rows)
        place = 2 * (2 * z + core)
        cut = [
            jnp.where(pick, mine[dp, pl.ds(place + k, 1), :], theirs[dp, pl.ds(place + k, 1), :])
            for k in range(2)
        ]
        blocks[pl.ds(e, 1), :] = jnp.concatenate(cut, axis=1)


def finish(queries, mine, theirs):
    return pl.pallas_call(
        finish_kernel,
        in_specs=[vmem()] * 3,
        out_specs=[vmem()] * 2,
        out_shape=[
            jax.ShapeDtypeStruct((2, 2 * mine.shape[2]), F32),
            jax.ShapeDtypeStruct((2, queries.shape[0]), F32),
        ],
        compiler_params=params(),
        name="finish",
    )(queries.reshape(1, -1), mine, theirs)


SWAP = [(0, 1), (1, 0)]


def body(acts, grads, proj_in, proj_out, lengths, queries):
    seq = acts.shape[1]
    depth = lax.axis_size("z")
    groups = lax.axis_size("x") * lax.axis_size("y")
    core = lax.axis_index("core")
    part = project(
        grads.reshape(-1, grads.shape[2]), acts.reshape(-1, acts.shape[2]), proj_out.T, proj_in.T, seq
    ).reshape(acts.shape[0], seq, -1)
    received = lax.ppermute(lax.dynamic_index_in_dim(part, 1 - core, 0, False), "core", SWAP)
    rows = lax.dynamic_index_in_dim(part, core, 0, False) + received
    rows = rows.reshape(depth, seq // depth, rows.shape[1])
    pieces = exchange(rows, "z", Z_ORDER)
    spread = outer(lengths, pieces, seq ** (-0.5))
    parts = exchange(spread, "z", Z_ORDER)
    own = total(parts)
    copies = jnp.broadcast_to(own[None], (groups,) + own.shape)
    gathered = exchange(copies, ("x", "y"), XY_ORDER)
    received = lax.ppermute(gathered, "core", SWAP)
    return tuple(finish(queries, gathered, received))


def solution(mesh):
    devices = mesh.devices.reshape(4, 4, 8, 2)
    dp, tensor = ("x", "y"), ("z", "core")
    return jax.shard_map(
        body,
        mesh=Mesh(devices, dp + tensor),
        in_specs=(
            P(dp, None, tensor),
            P(dp, None, tensor),
            P(tensor, None),
            P(tensor, None),
            P(dp),
            P(),
        ),
        out_specs=(P(dp, tensor), P(dp, None)),
        check_vma=False,
    )
```

```python
import functools

import jax
import jax.numpy as jnp
from jax import lax
from jax.experimental import pallas as pl
from jax.experimental.pallas import tpu as pltpu
from jax.sharding import Mesh, PartitionSpec as P

F32 = jnp.float32
HIGHEST = lax.Precision.HIGHEST
VMEM_BYTES = 24 * 1024 * 1024
NT = (((1,), (1,)), ((), ()))
TN = (((0,), (0,)), ((), ()))
Z_ORDER = (4, 0, 1, 7, 2, 6, 3, 5)
XY_ORDER = (10, 11, 12, 13, 14, 15, 0, 1, 2, 3, 4, 5, 6, 7, 8, 9)


def place_in(order, index):
    return sum(jnp.where(index == held, place, 0) for place, held in enumerate(order))


def exchange(x, axes, order):
    return lax.all_to_all(x, axes, 0, 0, axis_index_groups=[list(order)])


def vmem():
    return pl.BlockSpec(memory_space=pltpu.VMEM)


def params():
    return pltpu.CompilerParams(vmem_limit_bytes=VMEM_BYTES)


def in_hbm(x):
    return pltpu.with_memory_space_constraint(x, pltpu.HBM)


def project_kernel(grads, acts, w_out, w_in, out):
    rank = w_out.shape[0]
    out[:, rank:] = lax.dot_general(acts[...], w_in[...], NT, preferred_element_type=F32)
    out[:, :rank] = lax.dot_general(grads[...], w_out[...], NT, preferred_element_type=F32)


def project(grads, acts, w_out, w_in, tile):
    rows, width_out = grads.shape
    width_in = acts.shape[1]
    rank = w_out.shape[0]
    return pl.pallas_call(
        project_kernel,
        grid=(rows // tile,),
        in_specs=[
            pl.BlockSpec((tile, width_out), lambda r: (r, 0)),
            pl.BlockSpec((tile, width_in), lambda r: (r, 0)),
            pl.BlockSpec((rank, width_out), lambda r: (0, 0)),
            pl.BlockSpec((rank, width_in), lambda r: (0, 0)),
        ],
        out_specs=pl.BlockSpec((tile, 2 * rank), lambda r: (r, 0)),
        out_shape=jax.ShapeDtypeStruct((rows, 2 * rank), F32),
        compiler_params=params(),
        cost_estimate=pl.CostEstimate(
            flops=2 * rows * rank * (width_in + width_out),
            bytes_accessed=2 * (rows + rank) * (width_in + width_out) + 8 * rows * rank,
            transcendentals=0,
        ),
        name="project",
    )(in_hbm(grads), in_hbm(acts), in_hbm(w_out), in_hbm(w_in))


def outer_kernel(scale, lengths, pieces, out, square):
    rows = jnp.sum(pieces[...], axis=0)
    tokens, width = rows.shape
    rank = width // 2
    core = lax.axis_index("core")
    chunk = place_in(Z_ORDER, lax.axis_index("z"))
    count = jnp.where(core == 0, lengths[:, :1], lengths[:, 1:2])
    token = lax.broadcasted_iota(jnp.int32, (tokens, rank), 0) + chunk * tokens
    keep = (token < count).astype(F32)
    square[...] = scale * lax.dot_general(
        rows[:, :rank] * keep, rows[:, rank:], TN, precision=HIGHEST, preferred_element_type=F32
    )
    even = square[pl.ds(0, rank // 2, stride=2), :]
    odd = square[pl.ds(1, rank // 2, stride=2), :]
    flat = jnp.concatenate([even, odd], axis=1)
    out[...] = jnp.broadcast_to(flat[None], out.shape)


def outer(lengths, pieces, scale):
    shards, _, width = pieces.shape
    rank = width // 2
    return pl.pallas_call(
        functools.partial(outer_kernel, scale),
        in_specs=[vmem(), vmem()],
        out_specs=vmem(),
        out_shape=jax.ShapeDtypeStruct((shards, rank // 2, width), F32),
        scratch_shapes=[pltpu.VMEM((rank, rank), F32)],
        compiler_params=params(),
        name="outer",
    )(lengths.reshape(1, -1), pieces)


def total_kernel(pieces, own):
    own[...] = jnp.sum(pieces[...], axis=0)


def total(pieces):
    return pl.pallas_call(
        total_kernel,
        in_specs=[vmem()],
        out_specs=vmem(),
        out_shape=jax.ShapeDtypeStruct(pieces.shape[1:], F32),
        compiler_params=params(),
        name="total",
    )(pieces)


def chosen(queries, core, groups):
    held = lax.broadcasted_iota(jnp.int32, (groups, queries.shape[1]), 0) + XY_ORDER[0]
    group = jnp.where(held >= groups, held - groups, held)
    return (2 * group + core == queries[...]).astype(F32)


def dot_with(blocks, own, select):
    dots = jnp.sum(jnp.sum(blocks * own[None], axis=1), axis=1, keepdims=True)
    return jnp.sum(dots * select, axis=0, keepdims=True)


def own_place():
    return place_in(XY_ORDER, lax.axis_index("x") * lax.axis_size("y") + lax.axis_index("y"))


def begin_kernel(queries, mine, out):
    select = chosen(queries, lax.axis_index("core"), mine.shape[0])
    out[...] = dot_with(mine[...], mine[own_place()], select)


def begin(queries, mine):
    return pl.pallas_call(
        begin_kernel,
        in_specs=[vmem()] * 2,
        out_specs=vmem(),
        out_shape=jax.ShapeDtypeStruct((1, queries.shape[0]), F32),
        compiler_params=params(),
        name="begin",
    )(queries.reshape(1, -1), mine)


def finish_kernel(queries, begun, mine, theirs, blocks, scores):
    z, core = lax.axis_index("z"), lax.axis_index("core")
    groups, rows, _ = mine.shape
    dp = own_place()
    select = chosen(queries, core, groups)
    select_other = chosen(queries, 1 - core, groups)
    first, second = mine[...], theirs[...]
    my_row = begun[...] + dot_with(second, mine[dp], select_other)
    their_row = dot_with(first, theirs[dp], select) + dot_with(second, theirs[dp], select_other)
    place = 2 * (2 * z + core)
    for e in range(2):
        pick = core == e
        scores[pl.ds(e, 1), :] = jnp.where(pick, my_row, their_row) / (2 * rows)
        cut = [
            jnp.where(pick, mine[dp, pl.ds(place + k, 1), :], theirs[dp, pl.ds(place + k, 1), :])
            for k in range(2)
        ]
        blocks[pl.ds(e, 1), :] = jnp.concatenate(cut, axis=1)


def finish(queries, begun, mine, theirs):
    return pl.pallas_call(
        finish_kernel,
        in_specs=[vmem()] * 4,
        out_specs=[vmem()] * 2,
        out_shape=[
            jax.ShapeDtypeStruct((2, 2 * mine.shape[2]), F32),
            jax.ShapeDtypeStruct((2, queries.shape[0]), F32),
        ],
        compiler_params=params(),
        name="finish",
    )(queries.reshape(1, -1), begun, mine, theirs)


SWAP = [(0, 1), (1, 0)]


def body(acts, grads, proj_in, proj_out, lengths, queries):
    seq = acts.shape[1]
    depth = lax.axis_size("z")
    groups = lax.axis_size("x") * lax.axis_size("y")
    core = lax.axis_index("core")
    part = project(
        grads.reshape(-1, grads.shape[2]), acts.reshape(-1, acts.shape[2]), proj_out.T, proj_in.T, seq
    ).reshape(acts.shape[0], seq, -1)
    received = lax.ppermute(lax.dynamic_index_in_dim(part, 1 - core, 0, False), "core", SWAP)
    rows = lax.dynamic_index_in_dim(part, core, 0, False) + received
    rows = rows.reshape(depth, seq // depth, rows.shape[1])
    pieces = exchange(rows, "z", Z_ORDER)
    spread = outer(lengths, pieces, seq ** (-0.5))
    parts = exchange(spread, "z", Z_ORDER)
    own = total(parts)
    copies = jnp.broadcast_to(own[None], (groups,) + own.shape)
    gathered = exchange(copies, ("x", "y"), XY_ORDER)
    received = lax.ppermute(gathered, "core", SWAP)
    return tuple(finish(queries, begin(queries, gathered), gathered, received))


def solution(mesh):
    devices = mesh.devices.reshape(4, 4, 8, 2)
    dp, tensor = ("x", "y"), ("z", "core")
    return jax.shard_map(
        body,
        mesh=Mesh(devices, dp + tensor),
        in_specs=(
            P(dp, None, tensor),
            P(dp, None, tensor),
            P(tensor, None),
            P(tensor, None),
            P(dp),
            P(),
        ),
        out_specs=(P(dp, tensor), P(dp, None)),
        check_vma=False,
    )
```
